256 devices in a mesh: col: 128 (over x, y, z), layer: 2 (over core).
Axes of the slice: x: 4, y: 4, z: 8, core: 2. Of those that a mesh axis runs over, the one named last changes fastest.
Arguments:
- screens: float32 [2, 8192, 8192], P('layer', 'col'), may hold values from -12 to 12
- strips: float32 [2, 32, 8192], P('layer'), may hold values from -12 to 12
- wind_cols: int32 [2], replicated, may hold values from 1 to 32, as said below
- wind_rows: int32 [2], replicated, may hold values from -1024 to 1024
- heights: int32 [2], replicated, may hold values from 64 to 256
Outputs:
- pupil_field: float32 [2, 8192, 8192], P(None, ('col', 'layer'))
- next_screens: float32 [2, 8192, 8192], P('layer', 'col')
The draws below stay inside these ranges and needn't reach their ends.
Inputs may be any that keep to these rules, and one draw needn't show every extreme that they name: `wind_cols`: the layers move by distinct numbers of columns, and some layer moves by exactly 32.
All inputs are finite; a program needn't handle non-finite values.
Results may differ from the reference program's by a relative error of at most 0.00022.
Values sent between devices are 32-bit elements; how exact they have to be, the bound alone decides.
A program may use at most 128 MiB of HBM per device.

```python
import math
import jax
import jax.numpy as jnp
from jax import lax

N = 8192
VMAX = 32
LAYERS = 2
SPAN = 64


def draw_wind_cols(key, part):
    key = jax.random.fold_in(key, 11)
    pick_key, order_key = jax.random.split(key)
    others = jax.random.permutation(pick_key, VMAX - 1)[:LAYERS - 1] + 1
    values = jnp.concatenate([others.astype(jnp.int32), jnp.full((1,), VMAX, jnp.int32)])
    return jax.random.permutation(order_key, values).astype(jnp.int32)


def block_scale(rng, extent, shards, least, top_value):
    gain = 1.0
    for position, shards_of in shards:
        steps = jax.random.uniform(jax.random.fold_in(jax.random.fold_in(rng, 6), position), (shards_of,), jnp.float32, least / len(shards), top_value / len(shards))
        gain = gain * jnp.repeat(jnp.exp(steps), extent[position] // shards_of).reshape((-1,) + (1,) * (len(extent) - 1 - position))
    return gain


def centred(key, extent, width, reach, shards=(), kind=jnp.bfloat16):
    loudness = block_scale(key, extent, shards, -0.22, 0.18) if shards else 1.0
    result = jax.random.normal(key, extent, jnp.float32) * width * loudness
    return jnp.minimum(jnp.maximum(result, -reach), reach).astype(kind)


def setup_inputs(seed: int = 0) -> dict:
    key_of = jax.random.split(jax.random.key(seed), 6)
    return {
        "screens": centred(key_of[0], (LAYERS, N, N), 2.0, 12.0, ((0, 2), (1, 128)), jnp.float32),
        "strips": centred(key_of[1], (LAYERS, VMAX, N), 2.0, 12.0, ((0, 2),), jnp.float32),
        "wind_cols": draw_wind_cols(jax.random.fold_in(key_of[5], 71), 0),
        "wind_rows": jax.random.randint(key_of[3], (LAYERS,), -(N // 8), N // 8 + 1).astype(jnp.int32),
        "heights": jax.random.randint(key_of[4], (LAYERS,), SPAN, 4 * SPAN + 1).astype(jnp.int32),
    }


def fresnel_angle(frequency, distance, size):
    signed = jnp.where(frequency < size // 2, frequency, frequency - size)
    square = signed * signed
    high = square // size
    low = square % size
    count = (((distance * high) % size) * size + distance * low) % (size * size)
    return (2.0 * math.pi / (size * size)) * count.astype(jnp.float32)


def reference(screens, strips, wind_cols, wind_rows, heights):
    moved = []
    for layer in range(LAYERS):
        extended = jnp.concatenate([strips[layer], screens[layer]], axis=0)
        start = (VMAX - wind_cols[layer]).astype(jnp.int32)
        window = lax.dynamic_slice_in_dim(extended, start, N, 0)
        moved.append(jnp.roll(window, wind_rows[layer], axis=1))
    next_screens = jnp.stack(moved)
    frequency = jnp.arange(N, dtype=jnp.int32)
    field = jnp.exp(1j * next_screens[0])
    for layer in range(LAYERS):
        if layer > 0:
            field = field * jnp.exp(1j * next_screens[layer])
        angle = fresnel_angle(frequency, heights[layer], N)
        total = angle[:, None] + angle[None, :]
        spectrum = jnp.fft.fft2(field) * jnp.exp(-1j * total)
        field = jnp.fft.ifft2(spectrum)
    pupil_field = jnp.stack([jnp.real(field), jnp.imag(field)]).astype(jnp.float32)
    return pupil_field, next_screens
```

```python
import functools
import math

import jax
import jax.numpy as jnp
import numpy as np
from jax import lax
from jax.experimental import pallas as pl
from jax.experimental.pallas import tpu as pltpu
from jax.sharding import PartitionSpec as P

MESH = pl.DeviceIdType.MESH
F32 = jnp.float32
BF16 = jnp.bfloat16

SIZE = 8192
LANES = 128
SPAN = 64
REACH = 32
CHIPS = 128
DEVICES = 256
STEPS = 8


def cut(table):
    high = table.astype(np.float32).astype(BF16)
    low = (table - high.astype(np.float64)).astype(np.float32).astype(BF16)
    return high, low


def dft(count, sign):
    index = np.arange(count)
    return np.exp(sign * 2j * np.pi * (np.outer(index, index) % count) / count)


def left_complex(table):
    return np.block([[table.real, -table.imag], [table.imag, table.real]])


def right_complex(table):
    return np.block([[table.real, table.imag], [-table.imag, table.real]])


def left_half(table):
    high, low = cut(left_complex(table))
    return np.block([[high, high], [low, np.zeros_like(low)]])


def left_full(table):
    high, low = cut(left_complex(table))
    return np.concatenate([high, low, high], 1)


def right_full(table):
    high, low = cut(right_complex(table))
    return np.concatenate([high, low, high], 0)


def tables_y():
    twiddle = np.exp(-2j * np.pi * np.outer(np.arange(64), np.arange(128)) / SIZE)
    return [
        left_half(dft(64, -1)),
        left_half(dft(64, 1)),
        right_full(dft(128, -1)),
        right_full(dft(128, 1)),
        np.stack([twiddle.real, twiddle.imag]).astype(np.float32),
    ]


def tables_x():
    twiddle = np.exp(-2j * np.pi * np.outer(np.arange(128), np.arange(64)) / SIZE)
    twiddle = np.concatenate([twiddle, twiddle], 1)
    pair = np.eye(2)
    return [
        left_full(dft(128, -1)),
        left_full(dft(128, 1)),
        right_full(np.kron(pair, dft(64, -1))),
        right_full(np.kron(pair, dft(64, 1))),
        np.stack([twiddle.real, twiddle.imag]).astype(np.float32),
    ]


def wave(angle):
    square = angle * angle
    sine = -1.9515295891e-4 * square + 8.3321608736e-3
    sine = sine * square - 1.6666654611e-1
    sine = sine * square * angle + angle
    cosine = 2.443315711809948e-5 * square - 1.388731625493765e-3
    cosine = cosine * square + 4.166664568298827e-2
    cosine = cosine * square * square - 0.5 * square + 1.0
    return cosine, sine


def turned(cosine, sine, quarter):
    odd = (quarter & 1) == 1
    first = jnp.where(odd, sine, cosine)
    second = jnp.where(odd, cosine, sine)
    first = jnp.where(((quarter + 1) & 2) == 2, -first, first)
    second = jnp.where((quarter & 2) == 2, -second, second)
    return first, second


def cos_sin(angle):
    count = jnp.floor(angle * (2.0 / math.pi) + 0.5)
    rest = angle - count * 1.5703125
    rest = rest - count * 4.837512969970703125e-4
    rest = rest - count * 7.54978995489188216e-8
    cosine, sine = wave(rest)
    return turned(cosine, sine, count.astype(jnp.int32))


def symbol(frequency, distance, shift):
    signed = jnp.where(frequency < SIZE // 2, frequency, frequency - SIZE)
    count = (distance * signed * signed + shift * signed * SIZE) & (SIZE * SIZE - 1)
    unit = SIZE * SIZE // 4
    quarter = (count + unit // 2) // unit
    rest = (count - quarter * unit).astype(F32) * (2.0 * math.pi / (SIZE * SIZE))
    cosine, sine = wave(rest)
    cosine, sine = turned(cosine, sine, quarter)
    return cosine * (1.0 / SIZE), sine * (-1.0 / SIZE)


def split(value):
    high = value.astype(BF16)
    low = (value - high.astype(F32)).astype(BF16)
    return high, low


def dot(left, right):
    return jnp.dot(left, right, preferred_element_type=F32)


def apply_left_half(table, value):
    high, low = split(value)
    both = dot(table, jnp.concatenate([high, low], 0))
    rows = both.shape[0] // 2
    return both[:rows] + both[rows:]


def apply_left(table, value):
    high, low = split(value)
    return dot(table, jnp.concatenate([high, high, low], 0))


def apply_right(value, table):
    high, low = split(value)
    return dot(jnp.concatenate([high, high, low], 1), table)


def times(real, imag, other_real, other_imag):
    return (
        real * other_real - imag * other_imag,
        real * other_imag + imag * other_real,
    )


def symbol_y(ref, distance, shift):
    rows = lax.broadcasted_iota(jnp.int32, (64, 128), 0)
    lanes = lax.broadcasted_iota(jnp.int32, (64, 128), 1)
    ref[0], ref[1] = symbol(rows + 64 * lanes, distance, shift)


def symbol_x(ref, distance, shift):
    rows = lax.broadcasted_iota(jnp.int32, (128, 128), 0)
    lanes = lax.broadcasted_iota(jnp.int32, (128, 128), 1)
    ref[0], ref[1] = symbol(rows + 128 * (lanes % 64), distance, shift)


def along_y(src, dst, width, tables, phase):
    fwd_left, inv_left, fwd_right, inv_right, twiddle = tables
    together = 4

    def body(group, carry):
        first = group * together
        fields = []
        for i in range(together):
            rows = pl.ds(first + i, 64, stride=width)
            fields.append(jnp.concatenate([src[0, rows, :], src[1, rows, :]], 0))
        value = apply_left_half(fwd_left[...], jnp.concatenate(fields, 1))
        tw_real, tw_imag = twiddle[0], twiddle[1]
        pieces = []
        for i in range(together):
            lanes = slice(i * 128, (i + 1) * 128)
            pieces.append(
                jnp.concatenate(
                    times(value[:64, lanes], value[64:, lanes], tw_real, tw_imag), 1
                )
            )
        value = apply_right(jnp.concatenate(pieces, 0), fwd_right[...])
        ph_real, ph_imag = phase[0], phase[1]
        pieces = []
        for i in range(together):
            rows = slice(i * 64, (i + 1) * 64)
            pieces.append(
                jnp.concatenate(
                    times(value[rows, :128], value[rows, 128:], ph_real, ph_imag), 1
                )
            )
        value = apply_right(jnp.concatenate(pieces, 0), inv_right[...])
        fields = []
        for i in range(together):
            rows = slice(i * 64, (i + 1) * 64)
            fields.append(
                jnp.concatenate(
                    times(value[rows, :128], value[rows, 128:], tw_real, -tw_imag), 0
                )
            )
        value = apply_left_half(inv_left[...], jnp.concatenate(fields, 1))
        for i in range(together):
            rows = pl.ds(first + i, 64, stride=width)
            lanes = slice(i * 128, (i + 1) * 128)
            dst[0, rows, :] = value[:64, lanes]
            dst[1, rows, :] = value[64:, lanes]
        return carry

    lax.fori_loop(0, width // together, body, 0)


def along_x(fields, tables, phase):
    fwd_left, inv_left, fwd_right, inv_right, twiddle = tables
    tw_real, tw_imag = twiddle[0], twiddle[1]
    value = jnp.concatenate([jnp.concatenate(pair, 0) for pair in fields], 1)
    value = apply_left(fwd_left[...], value)
    pieces = []
    for i in range(2):
        lanes = slice(i * 128, (i + 1) * 128)
        pieces.append(
            jnp.concatenate(
                times(value[:128, lanes], value[128:, lanes], tw_real, tw_imag), 1
            )
        )
    value = apply_right(jnp.concatenate(pieces, 0), fwd_right[...])
    ph_real, ph_imag = phase[0], phase[1]
    pieces = []
    for i in range(2):
        rows = slice(i * 128, (i + 1) * 128)
        pieces.append(
            jnp.concatenate(
                times(value[rows, :128], value[rows, 128:], ph_real, ph_imag), 1
            )
        )
    value = apply_right(jnp.concatenate(pieces, 0), inv_right[...])
    pieces = []
    for i in range(2):
        rows = slice(i * 128, (i + 1) * 128)
        pieces.append(
            jnp.concatenate(
                times(value[rows, :128], value[rows, 128:], tw_real, -tw_imag), 0
            )
        )
    value = apply_left(inv_left[...], jnp.concatenate(pieces, 1))
    return [
        (value[:128, i * 128 : (i + 1) * 128], value[128:, i * 128 : (i + 1) * 128])
        for i in range(2)
    ]


def target_of(chip, step):
    offset = (step * 37) % CHIPS
    x = (chip // 32 + offset // 32) % 4
    y = ((chip // 8) % 4 + (offset // 8) % 4) % 4
    z = (chip % 8 + offset % 8) % 8
    return x * 32 + y * 8 + z


def send_all(chip, core, source, landing, send_sem, recv_sem):
    def one(step, carry):
        goal = target_of(chip, step)
        for goal_core in range(2):
            own = jnp.logical_and(step == 0, core == goal_core)

            @pl.when(jnp.logical_not(own))
            def _():
                pltpu.make_async_remote_copy(
                    source(goal, goal_core),
                    landing,
                    send_sem,
                    recv_sem,
                    device_id=(goal, goal_core),
                    device_id_type=MESH,
                ).start()

            @pl.when(own)
            def _():
                pltpu.make_async_copy(
                    source(goal, goal_core), landing, recv_sem
                ).start()

        return carry

    lax.fori_loop(0, CHIPS, one, 0)


def drain(view, sem):
    pltpu.make_async_copy(view, view, sem).wait()


def middle_kernel(
    heights,
    wind_cols,
    wind_rows,
    screen,
    strip,
    y0, y1, y2, y3, y4,
    x0, x1, x2, x3, x4,
    out,
    work,
    field_out,
    field_in,
    screen_out,
    screen_in,
    back_out,
    back_in,
    phase_y,
    phase_a,
    phase_b,
    field_send,
    field_recv,
    screen_send,
    screen_recv,
    back_send,
    back_recv,
):
    chip = lax.axis_index("col")
    core = lax.axis_index("layer")
    device = chip * 2 + core
    tables_of_y = (y0, y1, y2, y3, y4)
    tables_of_x = (x0, x1, x2, x3, x4)

    barrier = pltpu.get_barrier_semaphore()

    def greet(step, carry):
        goal = target_of(chip, step)

        @pl.when(step > 0)
        def _():
            pl.semaphore_signal(
                barrier, inc=1, device_id=(goal, core), device_id_type=MESH
            )

        pl.semaphore_signal(
            barrier, inc=1, device_id=(goal, 1 - core), device_id_type=MESH
        )
        return carry

    lax.fori_loop(0, CHIPS, greet, 0)

    least = REACH - wind_cols[core]
    row = lax.broadcasted_iota(jnp.int32, (REACH, LANES), 0)
    fresh = jnp.logical_and(chip == CHIPS - 1, row >= least)

    def unmoved(tile):
        lanes = pl.ds(pl.multiple_of(tile * LANES, LANES), LANES)
        edge = jnp.where(fresh, strip[0, :, lanes], screen[0, pl.ds(REACH, REACH), lanes])
        return jnp.concatenate([screen[0, pl.ds(0, REACH), lanes], edge], 0)

    @pl.when(core == 0)
    def _():
        symbol_y(phase_y, heights[0], wind_rows[0] - wind_rows[1])

        def start(tile, carry):
            rows = pl.ds(pl.multiple_of(tile * SPAN, SPAN), SPAN)
            work[0, rows, :], work[1, rows, :] = cos_sin(unmoved(tile))
            return carry

        lax.fori_loop(0, 64, start, 0)
        along_y(work, work, SPAN, tables_of_y, phase_y)

        def turn(tile, carry):
            rows = pl.ds(pl.multiple_of(tile * LANES, LANES), LANES)
            for part in range(2):
                lower = work[part, pl.ds(pl.multiple_of(tile * SPAN, SPAN), SPAN), :]
                upper = work[part, pl.ds(pl.multiple_of((tile + 32) * SPAN, SPAN), SPAN), :]
                field_out[part, rows, :] = jnp.concatenate([lower, upper], 0).T
            return carry

        lax.fori_loop(0, 32, turn, 0)

    @pl.when(core == 1)
    def _():
        def turn(tile, carry):
            rows = pl.ds(pl.multiple_of(tile * LANES, LANES), LANES)
            both = jnp.concatenate([unmoved(tile), unmoved(tile + 32)], 0)
            screen_out[rows, :] = both.T
            return carry

        lax.fori_loop(0, 32, turn, 0)

    pl.semaphore_wait(barrier, DEVICES - 1)

    slot = pl.ds(pl.multiple_of(chip * 8, 8), 8)

    @pl.when(core == 0)
    def _():
        def source(goal, goal_core):
            rows = pl.ds(pl.multiple_of((goal * 2 + goal_core) * 8, 8), 8)
            return field_out.reshape(2, 2, 2048, LANES).at[:, :, rows, :]

        send_all(chip, core, source, field_in.at[:, :, slot, :], field_send, field_recv)

    @pl.when(core == 1)
    def _():
        def source(goal, goal_core):
            rows = pl.ds(pl.multiple_of((goal * 2 + goal_core) * 8, 8), 8)
            return screen_out.reshape(2, 2048, LANES).at[:, rows, :]

        send_all(chip, core, source, screen_in.at[:, slot, :], screen_send, screen_recv)

    symbol_x(phase_a, heights[0], wind_cols[0] - wind_cols[1])
    symbol_x(phase_b, heights[1], wind_cols[1])

    drain(screen_in, screen_recv)
    drain(field_in, field_recv)

    lane = lax.broadcasted_iota(jnp.int32, (CHIPS, LANES), 1)
    odd = (lane // 32) % 2 == 1

    def rows_of(step, carry):
        rows = pl.ds(step, CHIPS, stride=STEPS)
        fields = [(field_in[0, i, rows, :], field_in[1, i, rows, :]) for i in range(2)]
        fields = along_x(fields, tables_of_x, phase_a)
        fields = [
            times(*fields[i], *cos_sin(screen_in[i, rows, :])) for i in range(2)
        ]
        fields = along_x(fields, tables_of_x, phase_b)
        for part in range(2):
            even_rows, odd_rows = fields[0][part], fields[1][part]
            back_out[part, 0, rows, :] = jnp.where(
                odd, pltpu.roll(odd_rows, 32, 1), even_rows
            )
            back_out[part, 1, rows, :] = jnp.where(
                odd, odd_rows, pltpu.roll(even_rows, 96, 1)
            )
        return carry

    lax.fori_loop(0, STEPS, rows_of, 0)

    def back_source(goal, goal_core):
        rows = pl.ds(pl.multiple_of(goal * 8, 8), 8)
        return back_out.at[:, goal_core, rows, :]

    own = pl.ds(pl.multiple_of(device * 8, 8), 8)
    send_all(chip, core, back_source, back_in.at[:, own, :], back_send, back_recv)

    @pl.when(core == 0)
    def _():
        sent = field_out.reshape(2, 2, 2048, LANES).at[:, :, pl.ds(0, 2040), :]
        drain(sent, field_send)

    @pl.when(core == 1)
    def _():
        sent = screen_out.reshape(2, 2048, LANES).at[:, pl.ds(0, 2040), :]
        drain(sent, screen_send)

    drain(back_in, back_recv)
    drain(back_in.at[:, pl.ds(0, 2040), :], back_send)
    out[...] = back_in[...]


def last_kernel(heights, wind_rows, came, y0, y1, y2, y3, y4, out, work, phase_y):
    symbol_y(phase_y, heights[1], wind_rows[1])

    def turn(tile, carry):
        rows = pl.ds(pl.multiple_of(tile * LANES, LANES), LANES)
        for part in range(2):
            turned_tile = came[part, rows, :].T
            for quarter in range(4):
                goal = pl.multiple_of((quarter * 16 + tile) * 32, 32)
                work[part, pl.ds(goal, 32), :] = turned_tile[quarter * 32 : quarter * 32 + 32]
        return carry

    lax.fori_loop(0, 16, turn, 0)
    along_y(work, work, 32, (y0, y1, y2, y3, y4), phase_y)

    def finish(tile, carry):
        lanes = pl.ds(pl.multiple_of(tile * LANES, LANES), LANES)
        rows = pl.ds(pl.multiple_of(tile * 32, 32), 32)
        for part in range(2):
            out[part, :, lanes] = work[part, rows, :]
        return carry

    lax.fori_loop(0, 64, finish, 0)


def passed_along(value, axis, steps):
    count = lax.axis_size(axis)
    return lax.ppermute(
        value, axis, [(source, source + steps) for source in range(count - steps)]
    )


def on_device(screens, strips, wind_cols, wind_rows, heights):
    group = lax.axis_index("layer")
    edge = screens[:, SPAN - REACH :, :]
    came = passed_along(edge, "col", 1)
    came = jnp.where(lax.axis_index("col") == 0, strips, came)
    extended = jnp.concatenate([came, screens], axis=1)
    start = REACH - wind_cols[group]
    window = lax.dynamic_slice_in_dim(extended[0], start, SPAN, 0)
    next_screens = jnp.roll(window, wind_rows[group], axis=1)[None]

    of_y = [jnp.asarray(table) for table in tables_y()]
    of_x = [jnp.asarray(table) for table in tables_x()]
    smem = pl.BlockSpec(memory_space=pltpu.SMEM)
    vmem = pl.BlockSpec(memory_space=pltpu.VMEM)
    middle = pl.pallas_call(
        middle_kernel,
        out_shape=jax.ShapeDtypeStruct((2, 2048, LANES), F32),
        in_specs=[smem] * 3 + [vmem] * 12,
        out_specs=vmem,
        scratch_shapes=[
            pltpu.VMEM((2, 4096, LANES), F32),
            pltpu.VMEM((2, 4096, LANES), F32),
            pltpu.VMEM((2, 2, 1024, LANES), F32),
            pltpu.VMEM((4096, LANES), F32),
            pltpu.VMEM((2, 1024, LANES), F32),
            pltpu.VMEM((2, 2, 1024, LANES), F32),
            pltpu.VMEM((2, 2048, LANES), F32),
            pltpu.VMEM((2, 64, LANES), F32),
            pltpu.VMEM((2, 128, LANES), F32),
            pltpu.VMEM((2, 128, LANES), F32),
        ]
        + [pltpu.SemaphoreType.DMA] * 6,
        compiler_params=pltpu.CompilerParams(
            collective_id=0, has_side_effects=True, vmem_limit_bytes=48 << 20
        ),
        name="middle",
    )(heights, wind_cols, wind_rows, screens, strips, *of_y, *of_x)
    field = pl.pallas_call(
        last_kernel,
        out_shape=jax.ShapeDtypeStruct((2, 32, SIZE), F32),
        in_specs=[smem] * 2 + [vmem] * 6,
        out_specs=vmem,
        scratch_shapes=[
            pltpu.VMEM((2, 2048, LANES), F32),
            pltpu.VMEM((2, 64, LANES), F32),
        ],
        compiler_params=pltpu.CompilerParams(vmem_limit_bytes=32 << 20),
        name="last",
    )(heights, wind_rows, middle, *of_y)
    return (field, next_screens)


def solution(mesh):
    placed = (P("layer", "col", None), P("layer", None, None), P(), P(), P())
    return jax.shard_map(
        on_device,
        mesh=mesh,
        in_specs=placed,
        out_specs=(P(None, ("col", "layer"), None), P("layer", "col", None)),
        check_vma=False,
    )
```

```python
import functools
import math

import jax
import jax.numpy as jnp
import numpy as np
from jax import lax
from jax.experimental import pallas as pl
from jax.experimental.pallas import tpu as pltpu
from jax.sharding import PartitionSpec as P

MESH = pl.DeviceIdType.MESH
F32 = jnp.float32
BF16 = jnp.bfloat16

SIZE = 8192
LANES = 128
SPAN = 64
REACH = 32
CHIPS = 128
DEVICES = 256
STEPS = 8


def cut(table):
    high = table.astype(np.float32).astype(BF16)
    low = (table - high.astype(np.float64)).astype(np.float32).astype(BF16)
    return high, low


def dft(count, sign):
    index = np.arange(count)
    return np.exp(sign * 2j * np.pi * (np.outer(index, index) % count) / count)


def left_complex(table):
    return np.block([[table.real, -table.imag], [table.imag, table.real]])


def right_complex(table):
    return np.block([[table.real, table.imag], [-table.imag, table.real]])


def left_half(table):
    high, low = cut(left_complex(table))
    return np.block([[high, high], [low, np.zeros_like(low)]])


def left_full(table):
    high, low = cut(left_complex(table))
    return np.concatenate([high, low, high], 1)


def right_full(table):
    high, low = cut(right_complex(table))
    return np.concatenate([high, low, high], 0)


def tables_y():
    twiddle = np.exp(-2j * np.pi * np.outer(np.arange(64), np.arange(128)) / SIZE)
    return [
        left_half(dft(64, -1)),
        left_half(dft(64, 1)),
        right_full(dft(128, -1)),
        right_full(dft(128, 1)),
        np.stack([twiddle.real, twiddle.imag]).astype(np.float32),
    ]


def tables_x():
    twiddle = np.exp(-2j * np.pi * np.outer(np.arange(128), np.arange(64)) / SIZE)
    twiddle = np.concatenate([twiddle, twiddle], 1)
    pair = np.eye(2)
    return [
        left_full(dft(128, -1)),
        left_full(dft(128, 1)),
        right_full(np.kron(pair, dft(64, -1))),
        right_full(np.kron(pair, dft(64, 1))),
        np.stack([twiddle.real, twiddle.imag]).astype(np.float32),
    ]


def wave(angle):
    square = angle * angle
    sine = -1.9515295891e-4 * square + 8.3321608736e-3
    sine = sine * square - 1.6666654611e-1
    sine = sine * square * angle + angle
    cosine = 2.443315711809948e-5 * square - 1.388731625493765e-3
    cosine = cosine * square + 4.166664568298827e-2
    cosine = cosine * square * square - 0.5 * square + 1.0
    return cosine, sine


def turned(cosine, sine, quarter):
    odd = (quarter & 1) == 1
    first = jnp.where(odd, sine, cosine)
    second = jnp.where(odd, cosine, sine)
    first = jnp.where(((quarter + 1) & 2) == 2, -first, first)
    second = jnp.where((quarter & 2) == 2, -second, second)
    return first, second


def cos_sin(angle):
    count = jnp.floor(angle * (2.0 / math.pi) + 0.5)
    rest = angle - count * 1.5703125
    rest = rest - count * 4.837512969970703125e-4
    rest = rest - count * 7.54978995489188216e-8
    cosine, sine = wave(rest)
    return turned(cosine, sine, count.astype(jnp.int32))


def symbol(frequency, distance, shift):
    signed = jnp.where(frequency < SIZE // 2, frequency, frequency - SIZE)
    count = (distance * signed * signed + shift * signed * SIZE) & (SIZE * SIZE - 1)
    unit = SIZE * SIZE // 4
    quarter = (count + unit // 2) // unit
    rest = (count - quarter * unit).astype(F32) * (2.0 * math.pi / (SIZE * SIZE))
    cosine, sine = wave(rest)
    cosine, sine = turned(cosine, sine, quarter)
    return cosine * (1.0 / SIZE), sine * (-1.0 / SIZE)


def split(value):
    high = value.astype(BF16)
    low = (value - high.astype(F32)).astype(BF16)
    return high, low


def dot(left, right):
    return jnp.dot(left, right, preferred_element_type=F32)


def apply_left_half(table, value):
    high, low = split(value)
    both = dot(table, jnp.concatenate([high, low], 0))
    rows = both.shape[0] // 2
    return both[:rows] + both[rows:]


def apply_left(table, value):
    high, low = split(value)
    return dot(table, jnp.concatenate([high, high, low], 0))


def apply_right(value, table):
    high, low = split(value)
    return dot(jnp.concatenate([high, high, low], 1), table)


def times(real, imag, other_real, other_imag):
    return (
        real * other_real - imag * other_imag,
        real * other_imag + imag * other_real,
    )


def symbol_y(ref, distance, shift):
    rows = lax.broadcasted_iota(jnp.int32, (64, 128), 0)
    lanes = lax.broadcasted_iota(jnp.int32, (64, 128), 1)
    ref[0], ref[1] = symbol(rows + 64 * lanes, distance, shift)


def symbol_x(ref, distance, shift):
    rows = lax.broadcasted_iota(jnp.int32, (128, 128), 0)
    lanes = lax.broadcasted_iota(jnp.int32, (128, 128), 1)
    ref[0], ref[1] = symbol(rows + 128 * (lanes % 64), distance, shift)


def along_y(src, dst, width, tables, phase):
    fwd_left, inv_left, fwd_right, inv_right, twiddle = tables
    together = 16

    def body(group, carry):
        first = group * together
        fields = []
        for i in range(together):
            rows = pl.ds(first + i, 64, stride=width)
            fields.append(jnp.concatenate([src[0, rows, :], src[1, rows, :]], 0))
        value = apply_left_half(fwd_left[...], jnp.concatenate(fields, 1))
        tw_real, tw_imag = twiddle[0], twiddle[1]
        pieces = []
        for i in range(together):
            lanes = slice(i * 128, (i + 1) * 128)
            pieces.append(
                jnp.concatenate(
                    times(value[:64, lanes], value[64:, lanes], tw_real, tw_imag), 1
                )
            )
        value = apply_right(jnp.concatenate(pieces, 0), fwd_right[...])
        ph_real, ph_imag = phase[0], phase[1]
        pieces = []
        for i in range(together):
            rows = slice(i * 64, (i + 1) * 64)
            pieces.append(
                jnp.concatenate(
                    times(value[rows, :128], value[rows, 128:], ph_real, ph_imag), 1
                )
            )
        value = apply_right(jnp.concatenate(pieces, 0), inv_right[...])
        fields = []
        for i in range(together):
            rows = slice(i * 64, (i + 1) * 64)
            fields.append(
                jnp.concatenate(
                    times(value[rows, :128], value[rows, 128:], tw_real, -tw_imag), 0
                )
            )
        value = apply_left_half(inv_left[...], jnp.concatenate(fields, 1))
        for i in range(together):
            rows = pl.ds(first + i, 64, stride=width)
            lanes = slice(i * 128, (i + 1) * 128)
            dst[0, rows, :] = value[:64, lanes]
            dst[1, rows, :] = value[64:, lanes]
        return carry

    lax.fori_loop(0, width // together, body, 0)


def along_x(fields, tables, phase):
    fwd_left, inv_left, fwd_right, inv_right, twiddle = tables
    tw_real, tw_imag = twiddle[0], twiddle[1]
    value = jnp.concatenate([jnp.concatenate(pair, 0) for pair in fields], 1)
    value = apply_left(fwd_left[...], value)
    pieces = []
    for i in range(len(fields)):
        lanes = slice(i * 128, (i + 1) * 128)
        pieces.append(
            jnp.concatenate(
                times(value[:128, lanes], value[128:, lanes], tw_real, tw_imag), 1
            )
        )
    value = apply_right(jnp.concatenate(pieces, 0), fwd_right[...])
    ph_real, ph_imag = phase[0], phase[1]
    pieces = []
    for i in range(len(fields)):
        rows = slice(i * 128, (i + 1) * 128)
        pieces.append(
            jnp.concatenate(
                times(value[rows, :128], value[rows, 128:], ph_real, ph_imag), 1
            )
        )
    value = apply_right(jnp.concatenate(pieces, 0), inv_right[...])
    pieces = []
    for i in range(len(fields)):
        rows = slice(i * 128, (i + 1) * 128)
        pieces.append(
            jnp.concatenate(
                times(value[rows, :128], value[rows, 128:], tw_real, -tw_imag), 0
            )
        )
    value = apply_left(inv_left[...], jnp.concatenate(pieces, 1))
    return [
        (value[:128, i * 128 : (i + 1) * 128], value[128:, i * 128 : (i + 1) * 128])
        for i in range(len(fields))
    ]


def target_of(chip, step):
    offset = (step * 37) % CHIPS
    x = (chip // 32 + offset // 32) % 4
    y = ((chip // 8) % 4 + (offset // 8) % 4) % 4
    z = (chip % 8 + offset % 8) % 8
    return x * 32 + y * 8 + z


def send_all(chip, core, source, landing, send_sem, recv_sem):
    def one(step, carry):
        goal = target_of(chip, step)
        for goal_core in range(2):
            own = jnp.logical_and(step == 0, core == goal_core)

            @pl.when(jnp.logical_not(own))
            def _():
                pltpu.make_async_remote_copy(
                    source(goal, goal_core),
                    landing,
                    send_sem,
                    recv_sem,
                    device_id=(goal, goal_core),
                    device_id_type=MESH,
                ).start()

            @pl.when(own)
            def _():
                pltpu.make_async_copy(
                    source(goal, goal_core), landing, recv_sem
                ).start()

        return carry

    lax.fori_loop(0, CHIPS, one, 0)


def drain(view, sem):
    pltpu.make_async_copy(view, view, sem).wait()


def tables_in(sources, places, sems, first):
    copies = [
        pltpu.make_async_copy(source, place, sems.at[first + i])
        for i, (source, place) in enumerate(zip(sources, places))
    ]
    for copy in copies:
        copy.start()
    return copies


def middle_kernel(
    heights,
    wind_cols,
    wind_rows,
    *refs,
):
    screen_hbm, strip_hbm = refs[:2]
    tables_hbm = refs[2:12]
    back_hbm, came_hbm = refs[12:14]
    screen, strip = refs[14:16]
    tables = refs[16:26]
    (
        work,
        field_out,
        field_in,
        screen_out,
        screen_in,
        back_out,
        back_in,
        came,
        phase_y,
        phase_a,
        phase_b,
        load_sems,
        field_send,
        field_recv,
        screen_send,
        screen_recv,
        back_send,
        back_recv,
        halo_send,
        halo_recv,
    ) = refs[26:]
    chip = lax.axis_index("col")
    core = lax.axis_index("layer")
    device = chip * 2 + core
    tables_of_y, tables_of_x = tables[:5], tables[5:]

    loads = tables_in(
        (screen_hbm.at[0], strip_hbm.at[0]) + tuple(tables_hbm),
        (screen, strip) + tuple(tables),
        load_sems,
        0,
    )

    barrier = pltpu.get_barrier_semaphore()

    def greet(step, carry):
        goal = target_of(chip, step)

        @pl.when(step > 0)
        def _():
            pl.semaphore_signal(
                barrier, inc=1, device_id=(goal, core), device_id_type=MESH
            )

        pl.semaphore_signal(
            barrier, inc=1, device_id=(goal, 1 - core), device_id_type=MESH
        )
        return carry

    lax.fori_loop(0, CHIPS, greet, 0)

    least = REACH - wind_cols[core]
    row = lax.broadcasted_iota(jnp.int32, (REACH, LANES), 0)
    fresh = jnp.logical_and(chip == CHIPS - 1, row >= least)

    def unmoved(tile):
        lanes = pl.ds(pl.multiple_of(tile * LANES, LANES), LANES)
        edge = jnp.where(fresh, strip[:, lanes], screen[pl.ds(REACH, REACH), lanes])
        return jnp.concatenate([screen[pl.ds(0, REACH), lanes], edge], 0)

    for copy in loads:
        copy.wait()

    @pl.when(core == 0)
    def _():
        symbol_y(phase_y, heights[0], wind_rows[0] - wind_rows[1])

        def start(tile, carry):
            rows = pl.ds(pl.multiple_of(tile * SPAN, SPAN), SPAN)
            work[0, rows, :], work[1, rows, :] = cos_sin(unmoved(tile))
            return carry

        lax.fori_loop(0, 64, start, 0)

    @pl.when(core == 1)
    def _():
        def turn(tile, carry):
            rows = pl.ds(pl.multiple_of(tile * LANES, LANES), LANES)
            both = jnp.concatenate([unmoved(tile), unmoved(tile + 32)], 0)
            screen_out[rows, :] = both.T
            return carry

        lax.fori_loop(0, 32, turn, 0)

    pl.semaphore_wait(barrier, DEVICES - 1)

    slot = pl.ds(pl.multiple_of(chip * 8, 8), 8)

    def pass_edge(tile, carry):
        lanes = pl.ds(pl.multiple_of(tile * LANES, LANES), LANES)
        pltpu.make_async_remote_copy(
            screen.at[pl.ds(REACH, REACH), lanes],
            came.at[:, lanes],
            halo_send,
            halo_recv,
            device_id=((chip + 1) % CHIPS, core),
            device_id_type=MESH,
        ).start()
        return carry

    @pl.when(core == 0)
    def _():
        lax.fori_loop(0, 64, pass_edge, 0)
        along_y(work, work, SPAN, tables_of_y, phase_y)

        def turn(tile, carry):
            rows = pl.ds(pl.multiple_of(tile * LANES, LANES), LANES)
            lower = pl.ds(pl.multiple_of(tile * SPAN, SPAN), SPAN)
            upper = pl.ds(pl.multiple_of((tile + 32) * SPAN, SPAN), SPAN)
            for part in range(2):
                both = jnp.concatenate([work[part, lower, :], work[part, upper, :]], 0)
                field_out[part, rows, :] = both.T
            return carry

        lax.fori_loop(0, 32, turn, 0)

        def send(half, carry):
            def source(goal, goal_core):
                rows = pl.ds(pl.multiple_of((goal * 2 + goal_core) * 8, 8), 8)
                return field_out.reshape(2, 2, 2048, LANES).at[:, half, rows, :]

            landing = field_in.at[:, half, slot, :]
            send_all(chip, core, source, landing, field_send, field_recv.at[half])
            return carry

        lax.fori_loop(0, 2, send, 0)

    @pl.when(core == 1)
    def _():
        def send(half, carry):
            def source(goal, goal_core):
                rows = pl.ds(pl.multiple_of((goal * 2 + goal_core) * 8, 8), 8)
                return screen_out.reshape(2, 2048, LANES).at[half, rows, :]

            landing = screen_in.at[half, slot, :]
            send_all(chip, core, source, landing, screen_send, screen_recv.at[half])
            return carry

        lax.fori_loop(0, 2, send, 0)
        lax.fori_loop(0, 64, pass_edge, 0)

    symbol_x(phase_a, heights[0], wind_cols[0] - wind_cols[1])
    symbol_x(phase_b, heights[1], wind_cols[1])

    lane = lax.broadcasted_iota(jnp.int32, (CHIPS, LANES), 1)
    odd = (lane // 32) % 2 == 1
    own = pl.ds(pl.multiple_of(device * 8, 8), 8)

    def half_of(half, carry):
        drain(screen_in.at[half], screen_recv.at[half])
        drain(field_in.at[:, half], field_recv.at[half])

        def rows_of(step, carry):
            slabs = [pl.ds(step * 4 + i, CHIPS, stride=STEPS) for i in range(4)]
            fields = [
                (field_in[0, half, rows, :], field_in[1, half, rows, :])
                for rows in slabs
            ]
            fields = along_x(fields, tables_of_x, phase_a)
            fields = [
                times(*field, *cos_sin(screen_in[half, rows, :]))
                for field, rows in zip(fields, slabs)
            ]
            fields = along_x(fields, tables_of_x, phase_b)
            for (real, imag), rows in zip(fields, slabs):
                back_out[half, 0, rows, :] = jnp.where(odd, pltpu.roll(imag, 32, 1), real)
                back_out[half, 1, rows, :] = jnp.where(odd, imag, pltpu.roll(real, 96, 1))
            return carry

        lax.fori_loop(0, 2, rows_of, 0)

        def source(goal, goal_core):
            rows = pl.ds(pl.multiple_of(goal * 8, 8), 8)
            return back_out.at[half, goal_core, rows, :]

        landing = back_in.at[half, own, :]
        send_all(chip, core, source, landing, back_send, back_recv.at[half])
        return carry

    lax.fori_loop(0, 2, half_of, 0)

    drain(came, halo_recv)
    keep = pltpu.make_async_copy(came, came_hbm, load_sems.at[0])
    keep.start()

    @pl.when(core == 0)
    def _():
        sent = field_out.reshape(2, 2, 2048, LANES).at[:, :, pl.ds(0, 2040), :]
        drain(sent, field_send)

    @pl.when(core == 1)
    def _():
        sent = screen_out.reshape(2, 2048, LANES).at[:, pl.ds(0, 2040), :]
        drain(sent, screen_send)

    drain(came, halo_send)
    stores = []
    for half in range(2):
        drain(back_in.at[half], back_recv.at[half])
        copy = pltpu.make_async_copy(
            back_in.at[half], back_hbm.at[half], load_sems.at[1 + half]
        )
        copy.start()
        stores.append(copy)
    drain(back_in.at[:, pl.ds(0, 2040), :], back_send)
    for copy in stores + [keep]:
        copy.wait()


def last_kernel(heights, wind_cols, wind_rows, *refs):
    back_hbm, came_hbm, screen_hbm, strip_hbm = refs[:4]
    tables_hbm = refs[4:9]
    out_hbm, next_hbm = refs[9:11]
    back, extended = refs[11:13]
    tables = refs[13:18]
    out, moved, work, phase_y, sems = refs[18:]
    chip = lax.axis_index("col")
    core = lax.axis_index("layer")

    loads = tables_in((back_hbm,) + tuple(tables_hbm), (back,) + tuple(tables), sems, 0)
    screen_copy = pltpu.make_async_copy(
        screen_hbm.at[0], extended.at[pl.ds(REACH, SPAN)], sems.at[6]
    )
    screen_copy.start()
    edge = extended.at[pl.ds(0, REACH)]

    @pl.when(chip == 0)
    def _():
        pltpu.make_async_copy(strip_hbm.at[0], edge, sems.at[7]).start()

    @pl.when(chip != 0)
    def _():
        pltpu.make_async_copy(came_hbm, edge, sems.at[7]).start()

    symbol_y(phase_y, heights[1], wind_rows[1])
    for copy in loads:
        copy.wait()

    def turn(tile, carry):
        rows = pl.ds(pl.multiple_of(tile * LANES, LANES), LANES)
        for half in range(2):
            tile_turned = back[half, rows, :].T
            for upper in range(2):
                goal = pl.multiple_of((upper * 32 + half * 16 + tile) * 32, 32)
                for part in range(2):
                    first = (upper * 2 + part) * 32
                    work[part, pl.ds(goal, 32), :] = tile_turned[first : first + 32]
        return carry

    lax.fori_loop(0, 16, turn, 0)
    along_y(work, work, 32, tables, phase_y)

    def finish(tile, carry):
        lanes = pl.ds(pl.multiple_of(tile * LANES, LANES), LANES)
        rows = pl.ds(pl.multiple_of(tile * 32, 32), 32)
        for part in range(2):
            out[part, :, lanes] = work[part, rows, :]
        return carry

    lax.fori_loop(0, 64, finish, 0)
    out_copy = pltpu.make_async_copy(out, out_hbm, sems.at[0])
    out_copy.start()

    screen_copy.wait()
    pltpu.make_async_copy(came_hbm, edge, sems.at[7]).wait()
    up = (SPAN + wind_cols[core]) % (SPAN + REACH)
    shift = wind_rows[core] & (SIZE - 1)
    tiles, within = shift // LANES, shift % LANES
    lane = lax.broadcasted_iota(jnp.int32, (SPAN, LANES), 1)

    def source(tile):
        lanes = pl.ds(pl.multiple_of(((tile - tiles) & 63) * LANES, LANES), LANES)
        block = pltpu.roll(extended[:, lanes], up, 0)[:SPAN]
        return pltpu.roll(block, within, 1)

    def move(tile, before):
        here = source(tile)
        lanes = pl.ds(pl.multiple_of(tile * LANES, LANES), LANES)
        moved[0, :, lanes] = jnp.where(lane >= within, here, before)
        return here

    lax.fori_loop(0, 64, move, source(-1))
    next_copy = pltpu.make_async_copy(moved, next_hbm, sems.at[1])
    next_copy.start()
    out_copy.wait()
    next_copy.wait()


def on_device(screens, strips, wind_cols, wind_rows, heights):
    of_y = [jnp.asarray(table) for table in tables_y()]
    of_x = [jnp.asarray(table) for table in tables_x()]
    smem = pl.BlockSpec(memory_space=pltpu.SMEM)
    anywhere = pl.BlockSpec(memory_space=pl.ANY)
    places_y = [pltpu.VMEM(table.shape, table.dtype) for table in of_y]
    places_x = [pltpu.VMEM(table.shape, table.dtype) for table in of_x]
    back, came = pl.pallas_call(
        middle_kernel,
        out_shape=(
            jax.ShapeDtypeStruct((2, 2048, LANES), F32),
            jax.ShapeDtypeStruct((REACH, SIZE), F32),
        ),
        in_specs=[smem] * 3 + [anywhere] * 12,
        out_specs=(anywhere, anywhere),
        scratch_shapes=[
            pltpu.VMEM((SPAN, SIZE), F32),
            pltpu.VMEM((REACH, SIZE), F32),
        ]
        + places_y
        + places_x
        + [
            pltpu.VMEM((2, 4096, LANES), F32),
            pltpu.VMEM((2, 4096, LANES), F32),
            pltpu.VMEM((2, 2, 1024, LANES), F32),
            pltpu.VMEM((4096, LANES), F32),
            pltpu.VMEM((2, 1024, LANES), F32),
            pltpu.VMEM((2, 2, 1024, LANES), F32),
            pltpu.VMEM((2, 2048, LANES), F32),
            pltpu.VMEM((REACH, SIZE), F32),
            pltpu.VMEM((2, 64, LANES), F32),
            pltpu.VMEM((2, 128, LANES), F32),
            pltpu.VMEM((2, 128, LANES), F32),
            pltpu.SemaphoreType.DMA((12,)),
            pltpu.SemaphoreType.DMA,
            pltpu.SemaphoreType.DMA((2,)),
            pltpu.SemaphoreType.DMA,
            pltpu.SemaphoreType.DMA((2,)),
            pltpu.SemaphoreType.DMA,
            pltpu.SemaphoreType.DMA((2,)),
            pltpu.SemaphoreType.DMA,
            pltpu.SemaphoreType.DMA,
        ],
        compiler_params=pltpu.CompilerParams(
            collective_id=0, has_side_effects=True, vmem_limit_bytes=60 << 20
        ),
        name="middle",
    )(heights, wind_cols, wind_rows, screens, strips, *of_y, *of_x)
    return pl.pallas_call(
        last_kernel,
        out_shape=(
            jax.ShapeDtypeStruct((2, 32, SIZE), F32),
            jax.ShapeDtypeStruct((1, SPAN, SIZE), F32),
        ),
        in_specs=[smem] * 3 + [anywhere] * 9,
        out_specs=(anywhere, anywhere),
        scratch_shapes=[
            pltpu.VMEM((2, 2048, LANES), F32),
            pltpu.VMEM((REACH + SPAN, SIZE), F32),
        ]
        + places_y
        + [
            pltpu.VMEM((2, 32, SIZE), F32),
            pltpu.VMEM((1, SPAN, SIZE), F32),
            pltpu.VMEM((2, 2048, LANES), F32),
            pltpu.VMEM((2, 64, LANES), F32),
            pltpu.SemaphoreType.DMA((8,)),
        ],
        compiler_params=pltpu.CompilerParams(vmem_limit_bytes=60 << 20),
        name="last",
    )(heights, wind_cols, wind_rows, back, came, screens, strips, *of_y)


def solution(mesh):
    placed = (P("layer", "col", None), P("layer", None, None), P(), P(), P())
    return jax.shard_map(
        on_device,
        mesh=mesh,
        in_specs=placed,
        out_specs=(P(None, ("col", "layer"), None), P("layer", "col", None)),
        check_vma=False,
    )
```

```python
import functools
import math

import jax
import jax.numpy as jnp
import numpy as np
from jax import lax
from jax.experimental import pallas as pl
from jax.experimental.pallas import tpu as pltpu
from jax.sharding import PartitionSpec as P

MESH = pl.DeviceIdType.MESH
F32 = jnp.float32
BF16 = jnp.bfloat16

SIZE = 8192
LANES = 128
SPAN = 64
REACH = 32
CHIPS = 128
DEVICES = 256
STEPS = 8
EARLY = 32
ORDER = (0, 1, 2, 3, 4, 5, 6, 7)


def cut(table):
    high = table.astype(np.float32).astype(BF16)
    low = (table - high.astype(np.float64)).astype(np.float32).astype(BF16)
    return high, low


def dft(count, sign):
    index = np.arange(count)
    return np.exp(sign * 2j * np.pi * (np.outer(index, index) % count) / count)


def left_complex(table):
    return np.block([[table.real, -table.imag], [table.imag, table.real]])


def right_complex(table):
    return np.block([[table.real, table.imag], [-table.imag, table.real]])


def left_half(table):
    high, low = cut(left_complex(table))
    return np.block([[high, high], [low, np.zeros_like(low)]])


def left_full(table):
    high, low = cut(left_complex(table))
    return np.concatenate([high, low, high], 1)


def right_full(table):
    high, low = cut(right_complex(table))
    return np.concatenate([high, low, high], 0)


def tables_y():
    twiddle = np.exp(-2j * np.pi * np.outer(np.arange(64), np.arange(128)) / SIZE)
    return [
        left_half(dft(64, -1)),
        left_half(dft(64, 1)),
        right_full(dft(128, -1)),
        right_full(dft(128, 1)),
        np.stack([twiddle.real, twiddle.imag]).astype(np.float32),
    ]


def tables_x():
    twiddle = np.exp(-2j * np.pi * np.outer(np.arange(128), np.arange(64)) / SIZE)
    twiddle = np.concatenate([twiddle, twiddle], 1)
    pair = np.eye(2)
    return [
        left_full(dft(128, -1)),
        left_full(dft(128, 1)),
        right_full(np.kron(pair, dft(64, -1))),
        right_full(np.kron(pair, dft(64, 1))),
        np.stack([twiddle.real, twiddle.imag]).astype(np.float32),
    ]


def wave(angle):
    square = angle * angle
    sine = -1.9515295891e-4 * square + 8.3321608736e-3
    sine = sine * square - 1.6666654611e-1
    sine = sine * square * angle + angle
    cosine = 2.443315711809948e-5 * square - 1.388731625493765e-3
    cosine = cosine * square + 4.166664568298827e-2
    cosine = cosine * square * square - 0.5 * square + 1.0
    return cosine, sine


def turned(cosine, sine, quarter):
    odd = (quarter & 1) == 1
    first = jnp.where(odd, sine, cosine)
    second = jnp.where(odd, cosine, sine)
    first = jnp.where(((quarter + 1) & 2) == 2, -first, first)
    second = jnp.where((quarter & 2) == 2, -second, second)
    return first, second


def cos_sin(angle):
    count = jnp.floor(angle * (2.0 / math.pi) + 0.5)
    rest = angle - count * 1.5703125
    rest = rest - count * 4.837512969970703125e-4
    rest = rest - count * 7.54978995489188216e-8
    cosine, sine = wave(rest)
    return turned(cosine, sine, count.astype(jnp.int32))


def symbol(frequency, distance, shift):
    signed = jnp.where(frequency < SIZE // 2, frequency, frequency - SIZE)
    count = (distance * signed * signed + shift * signed * SIZE) & (SIZE * SIZE - 1)
    unit = SIZE * SIZE // 4
    quarter = (count + unit // 2) // unit
    rest = (count - quarter * unit).astype(F32) * (2.0 * math.pi / (SIZE * SIZE))
    cosine, sine = wave(rest)
    cosine, sine = turned(cosine, sine, quarter)
    return cosine * (1.0 / SIZE), sine * (-1.0 / SIZE)


def split(value):
    high = value.astype(BF16)
    low = (value - high.astype(F32)).astype(BF16)
    return high, low


def dot(left, right):
    return jnp.dot(left, right, preferred_element_type=F32)


def apply_left_half(table, value):
    high, low = split(value)
    both = dot(table, jnp.concatenate([high, low], 0))
    rows = both.shape[0] // 2
    return both[:rows] + both[rows:]


def apply_left(table, value):
    high, low = split(value)
    return dot(table, jnp.concatenate([high, high, low], 0))


def apply_right(value, table):
    high, low = split(value)
    return dot(jnp.concatenate([high, high, low], 1), table)


def times(real, imag, other_real, other_imag):
    return (
        real * other_real - imag * other_imag,
        real * other_imag + imag * other_real,
    )


def symbol_y(ref, distance, shift):
    rows = lax.broadcasted_iota(jnp.int32, (64, 128), 0)
    lanes = lax.broadcasted_iota(jnp.int32, (64, 128), 1)
    ref[0], ref[1] = symbol(rows + 64 * lanes, distance, shift)


def symbol_x(ref, distance, shift):
    rows = lax.broadcasted_iota(jnp.int32, (128, 128), 0)
    lanes = lax.broadcasted_iota(jnp.int32, (128, 128), 1)
    ref[0], ref[1] = symbol(rows + 128 * (lanes % 64), distance, shift)


def along_y(src, dst, width, tables, phase):
    fwd_left, inv_left, fwd_right, inv_right, twiddle = tables
    together = 16

    def body(group, carry):
        first = group * together
        fields = []
        for i in range(together):
            rows = pl.ds(first + i, 64, stride=width)
            fields.append(jnp.concatenate([src[0, rows, :], src[1, rows, :]], 0))
        value = apply_left_half(fwd_left[...], jnp.concatenate(fields, 1))
        tw_real, tw_imag = twiddle[0], twiddle[1]
        pieces = []
        for i in range(together):
            lanes = slice(i * 128, (i + 1) * 128)
            pieces.append(
                jnp.concatenate(
                    times(value[:64, lanes], value[64:, lanes], tw_real, tw_imag), 1
                )
            )
        value = apply_right(jnp.concatenate(pieces, 0), fwd_right[...])
        ph_real, ph_imag = phase[0], phase[1]
        pieces = []
        for i in range(together):
            rows = slice(i * 64, (i + 1) * 64)
            pieces.append(
                jnp.concatenate(
                    times(value[rows, :128], value[rows, 128:], ph_real, ph_imag), 1
                )
            )
        value = apply_right(jnp.concatenate(pieces, 0), inv_right[...])
        fields = []
        for i in range(together):
            rows = slice(i * 64, (i + 1) * 64)
            fields.append(
                jnp.concatenate(
                    times(value[rows, :128], value[rows, 128:], tw_real, -tw_imag), 0
                )
            )
        value = apply_left_half(inv_left[...], jnp.concatenate(fields, 1))
        for i in range(together):
            rows = pl.ds(first + i, 64, stride=width)
            lanes = slice(i * 128, (i + 1) * 128)
            dst[0, rows, :] = value[:64, lanes]
            dst[1, rows, :] = value[64:, lanes]
        return carry

    lax.fori_loop(0, width // together, body, 0)


def along_x(fields, tables, phase):
    fwd_left, inv_left, fwd_right, inv_right, twiddle = tables
    tw_real, tw_imag = twiddle[0], twiddle[1]
    value = jnp.concatenate([jnp.concatenate(pair, 0) for pair in fields], 1)
    value = apply_left(fwd_left[...], value)
    pieces = []
    for i in range(len(fields)):
        lanes = slice(i * 128, (i + 1) * 128)
        pieces.append(
            jnp.concatenate(
                times(value[:128, lanes], value[128:, lanes], tw_real, tw_imag), 1
            )
        )
    value = apply_right(jnp.concatenate(pieces, 0), fwd_right[...])
    ph_real, ph_imag = phase[0], phase[1]
    pieces = []
    for i in range(len(fields)):
        rows = slice(i * 128, (i + 1) * 128)
        pieces.append(
            jnp.concatenate(
                times(value[rows, :128], value[rows, 128:], ph_real, ph_imag), 1
            )
        )
    value = apply_right(jnp.concatenate(pieces, 0), inv_right[...])
    pieces = []
    for i in range(len(fields)):
        rows = slice(i * 128, (i + 1) * 128)
        pieces.append(
            jnp.concatenate(
                times(value[rows, :128], value[rows, 128:], tw_real, -tw_imag), 0
            )
        )
    value = apply_left(inv_left[...], jnp.concatenate(pieces, 1))
    return [
        (value[:128, i * 128 : (i + 1) * 128], value[128:, i * 128 : (i + 1) * 128])
        for i in range(len(fields))
    ]


def every_chip(chip, visit):
    x, y, z = chip // 32, (chip // 8) % 4, chip % 8
    along_z = [(z + step) % 8 for step in ORDER]

    def plane(step, carry):
        base = ((x + step // 4) % 4) * 32 + ((y + step % 4) % 4) * 8
        for steps, place in zip(ORDER, along_z):
            visit(base + place, step == 0 if steps == 0 else None)
        return carry

    lax.fori_loop(0, 16, plane, 0)


def send_all(core, source, landing, send_sem, recv_sem):
    def remote(goal, goal_core):
        pltpu.make_async_remote_copy(
            source(goal, goal_core),
            landing,
            send_sem,
            recv_sem,
            device_id=(goal, goal_core),
            device_id_type=MESH,
        ).start()

    def visit(goal, own_chip):
        for goal_core in range(2):
            if own_chip is None:
                remote(goal, goal_core)
                continue
            own = jnp.logical_and(own_chip, core == goal_core)

            @pl.when(jnp.logical_not(own))
            def _():
                remote(goal, goal_core)

            @pl.when(own)
            def _():
                pltpu.make_async_copy(
                    source(goal, goal_core), landing, recv_sem
                ).start()

    return visit


def drain(view, sem):
    pltpu.make_async_copy(view, view, sem).wait()


def tables_in(sources, places, sems, first):
    copies = [
        pltpu.make_async_copy(source, place, sems.at[first + i])
        for i, (source, place) in enumerate(zip(sources, places))
    ]
    for copy in copies:
        copy.start()
    return copies


def middle_kernel(
    heights,
    wind_cols,
    wind_rows,
    *refs,
):
    screen_hbm, strip_hbm = refs[:2]
    tables_hbm = refs[2:12]
    out_hbm, came_hbm = refs[12:14]
    screen, strip = refs[14:16]
    tables = refs[16:26]
    (
        work,
        field_out,
        field_in,
        screen_out,
        screen_in,
        back_out,
        back_in,
        came,
        out,
        phase_y,
        phase_a,
        phase_b,
        load_sems,
        field_send,
        field_recv,
        screen_send,
        screen_recv,
        back_send,
        back_recv,
        halo_send,
        halo_recv,
    ) = refs[26:]
    chip = lax.axis_index("col")
    core = lax.axis_index("layer")
    device = chip * 2 + core
    tables_of_y, tables_of_x = tables[:5], tables[5:]

    loads = tables_in(
        (screen_hbm.at[0], strip_hbm.at[0]) + tuple(tables_hbm),
        (screen, strip) + tuple(tables),
        load_sems,
        0,
    )

    barrier = pltpu.get_barrier_semaphore()

    def greet(goal, own_chip):
        def signal(goal_core):
            pl.semaphore_signal(
                barrier, inc=1, device_id=(goal, goal_core), device_id_type=MESH
            )

        if own_chip is None:
            signal(core)
        else:
            pl.when(jnp.logical_not(own_chip))(lambda: signal(core))
        signal(1 - core)

    every_chip(chip, greet)

    least = REACH - wind_cols[core]
    row = lax.broadcasted_iota(jnp.int32, (REACH, LANES), 0)
    fresh = jnp.logical_and(chip == CHIPS - 1, row >= least)

    def unmoved(tile):
        lanes = pl.ds(pl.multiple_of(tile * LANES, LANES), LANES)
        edge = jnp.where(fresh, strip[:, lanes], screen[pl.ds(REACH, REACH), lanes])
        return jnp.concatenate([screen[pl.ds(0, REACH), lanes], edge], 0)

    for copy in loads:
        copy.wait()

    @pl.when(core == 0)
    def _():
        symbol_y(phase_y, heights[0], wind_rows[0] - wind_rows[1])

        def start(tile, carry):
            rows = pl.ds(pl.multiple_of(tile * SPAN, SPAN), SPAN)
            work[0, rows, :], work[1, rows, :] = cos_sin(unmoved(tile))
            return carry

        lax.fori_loop(0, 64, start, 0)

    @pl.when(core == 1)
    def _():
        def turn(tile, carry):
            rows = pl.ds(pl.multiple_of(tile * LANES, LANES), LANES)
            both = jnp.concatenate([unmoved(tile), unmoved(tile + 32)], 0)
            screen_out[rows, :] = both.T
            return carry

        lax.fori_loop(0, 32, turn, 0)

    pl.semaphore_wait(barrier, DEVICES - 1)

    slot = pl.ds(pl.multiple_of(chip * 8, 8), 8)

    def pass_edge(tile, carry):
        lanes = pl.ds(pl.multiple_of(tile * LANES, LANES), LANES)
        pltpu.make_async_remote_copy(
            screen.at[pl.ds(REACH, REACH), lanes],
            came.at[:, lanes],
            halo_send,
            halo_recv,
            device_id=((chip + 1) % CHIPS, core),
            device_id_type=MESH,
        ).start()
        return carry

    @pl.when(core == 0)
    def _():
        lax.fori_loop(0, EARLY, pass_edge, 0)
        along_y(work, work, SPAN, tables_of_y, phase_y)

        def turn(tile, carry):
            rows = pl.ds(pl.multiple_of(tile * LANES, LANES), LANES)
            lower = pl.ds(pl.multiple_of(tile * SPAN, SPAN), SPAN)
            upper = pl.ds(pl.multiple_of((tile + 32) * SPAN, SPAN), SPAN)
            for part in range(2):
                both = jnp.concatenate([work[part, lower, :], work[part, upper, :]], 0)
                field_out[part, rows, :] = both.T
            return carry

        lax.fori_loop(0, 32, turn, 0)

        def send(half, carry):
            def source(goal, goal_core):
                rows = pl.ds(pl.multiple_of((goal * 2 + goal_core) * 8, 8), 8)
                return field_out.reshape(2, 2, 2048, LANES).at[:, half, rows, :]

            landing = field_in.at[:, half, slot, :]
            every_chip(chip, send_all(core, source, landing, field_send, field_recv.at[half]))
            return carry

        lax.fori_loop(0, 2, send, 0)

    @pl.when(core == 1)
    def _():
        def send(half, carry):
            def source(goal, goal_core):
                rows = pl.ds(pl.multiple_of((goal * 2 + goal_core) * 8, 8), 8)
                return screen_out.reshape(2, 2048, LANES).at[half, rows, :]

            landing = screen_in.at[half, slot, :]
            every_chip(chip, send_all(core, source, landing, screen_send, screen_recv.at[half]))
            return carry

        lax.fori_loop(0, 2, send, 0)
        lax.fori_loop(0, EARLY, pass_edge, 0)

    symbol_x(phase_a, heights[0], wind_cols[0] - wind_cols[1])
    symbol_x(phase_b, heights[1], wind_cols[1])

    lane = lax.broadcasted_iota(jnp.int32, (CHIPS, LANES), 1)
    odd = (lane // 32) % 2 == 1
    own = pl.ds(pl.multiple_of(device * 8, 8), 8)

    def half_of(half, carry):
        drain(screen_in.at[half], screen_recv.at[half])
        drain(field_in.at[:, half], field_recv.at[half])

        def rows_of(step, carry):
            slabs = [pl.ds(step * 4 + i, CHIPS, stride=STEPS) for i in range(4)]
            fields = [
                (field_in[0, half, rows, :], field_in[1, half, rows, :])
                for rows in slabs
            ]
            fields = along_x(fields, tables_of_x, phase_a)
            fields = [
                times(*field, *cos_sin(screen_in[half, rows, :]))
                for field, rows in zip(fields, slabs)
            ]
            fields = along_x(fields, tables_of_x, phase_b)
            for (real, imag), rows in zip(fields, slabs):
                back_out[half, 0, rows, :] = jnp.where(odd, pltpu.roll(imag, 32, 1), real)
                back_out[half, 1, rows, :] = jnp.where(odd, imag, pltpu.roll(real, 96, 1))
            return carry

        lax.fori_loop(0, 2, rows_of, 0)

        def source(goal, goal_core):
            rows = pl.ds(pl.multiple_of(goal * 8, 8), 8)
            return back_out.at[half, goal_core, rows, :]

        landing = back_in.at[half, own, :]
        every_chip(chip, send_all(core, source, landing, back_send, back_recv.at[half]))
        return carry

    lax.fori_loop(0, 2, half_of, 0)

    lax.fori_loop(EARLY, 64, pass_edge, 0)

    symbol_y(phase_y, heights[1], wind_rows[1])

    def lanes_of(tile):
        return pl.ds(pl.multiple_of(tile * LANES, LANES), LANES)

    @pl.when(core == 0)
    def _():
        sent = field_out.reshape(2, 2, 2048, LANES).at[:, :, pl.ds(0, 2040), :]
        drain(sent, field_send)

    @pl.when(core == 1)
    def _():
        sent = screen_out.reshape(2, 2048, LANES).at[:, pl.ds(0, 2040), :]
        drain(sent, screen_send)

    for half in range(2):
        drain(back_in.at[half], back_recv.at[half])

        def turn_back(tile, carry):
            rows = pl.ds(pl.multiple_of(tile * LANES, LANES), LANES)
            tile_turned = back_in[half, rows, :].T
            for upper in range(2):
                goal = pl.multiple_of((upper * 32 + half * 16 + tile) * 32, 32)
                for part in range(2):
                    first = (upper * 2 + part) * 32
                    work[part, pl.ds(goal, 32), :] = tile_turned[first : first + 32]
            return carry

        lax.fori_loop(0, 16, turn_back, 0)
    along_y(work, work, 32, tables_of_y, phase_y)

    def finish(tile, carry):
        rows = pl.ds(pl.multiple_of(tile * 32, 32), 32)
        for part in range(2):
            out[part, :, lanes_of(tile)] = work[part, rows, :]
        return carry

    lax.fori_loop(0, 64, finish, 0)
    result = pltpu.make_async_copy(out, out_hbm, load_sems.at[1])
    result.start()

    drain(came, halo_recv)

    keep = pltpu.make_async_copy(came, came_hbm, load_sems.at[0])
    keep.start()
    drain(came, halo_send)
    drain(back_in.at[:, pl.ds(0, 2040), :], back_send)
    result.wait()
    keep.wait()


def last_kernel(wind_cols, wind_rows, *refs):
    field_hbm, came_hbm, screen_hbm, strip_hbm, out_hbm, next_hbm = refs[:6]
    extended, moved, field, sems = refs[6:]
    chip = lax.axis_index("col")
    core = lax.axis_index("layer")

    edge = extended.at[pl.ds(0, REACH)]
    screen_copy = pltpu.make_async_copy(
        screen_hbm.at[0], extended.at[pl.ds(REACH, SPAN)], sems.at[0]
    )
    screen_copy.start()

    @pl.when(chip == 0)
    def _():
        pltpu.make_async_copy(strip_hbm.at[0], edge, sems.at[1]).start()

    @pl.when(chip != 0)
    def _():
        pltpu.make_async_copy(came_hbm, edge, sems.at[1]).start()

    field_copy = pltpu.make_async_copy(field_hbm, field, sems.at[2])
    field_copy.start()
    screen_copy.wait()
    pltpu.make_async_copy(came_hbm, edge, sems.at[1]).wait()

    up = (SPAN + wind_cols[core]) % (SPAN + REACH)
    shift = wind_rows[core] & (SIZE - 1)
    tiles, within = shift // LANES, shift % LANES
    kept = lax.broadcasted_iota(jnp.int32, (SPAN, LANES), 1) >= within

    def source(tile):
        lanes = pl.ds(pl.multiple_of(((tile - tiles) & 63) * LANES, LANES), LANES)
        block = pltpu.roll(extended[:, lanes], up, 0)[:SPAN]
        return pltpu.roll(block, within, 1)

    def move(group, before):
        for i in range(8):
            tile = group * 8 + i
            here = source(tile)
            lanes = pl.ds(pl.multiple_of(tile * LANES, LANES), LANES)
            moved[0, :, lanes] = jnp.where(kept, here, before)
            before = here
        return before

    field_copy.wait()
    out_copy = pltpu.make_async_copy(field, out_hbm, sems.at[2])
    out_copy.start()
    lax.fori_loop(0, 8, move, source(-1))
    next_copy = pltpu.make_async_copy(moved, next_hbm, sems.at[3])
    next_copy.start()
    out_copy.wait()
    next_copy.wait()


def on_device(screens, strips, wind_cols, wind_rows, heights):
    of_y = [jnp.asarray(table) for table in tables_y()]
    of_x = [jnp.asarray(table) for table in tables_x()]
    smem = pl.BlockSpec(memory_space=pltpu.SMEM)
    anywhere = pl.BlockSpec(memory_space=pl.ANY)
    places_y = [pltpu.VMEM(table.shape, table.dtype) for table in of_y]
    places_x = [pltpu.VMEM(table.shape, table.dtype) for table in of_x]
    field, came = pl.pallas_call(
        middle_kernel,
        out_shape=(
            jax.ShapeDtypeStruct((2, REACH, SIZE), F32),
            jax.ShapeDtypeStruct((REACH, SIZE), F32),
        ),
        in_specs=[smem] * 3 + [anywhere] * 12,
        out_specs=(anywhere, anywhere),
        scratch_shapes=[
            pltpu.VMEM((SPAN, SIZE), F32),
            pltpu.VMEM((REACH, SIZE), F32),
        ]
        + places_y
        + places_x
        + [
            pltpu.VMEM((2, 4096, LANES), F32),
            pltpu.VMEM((2, 4096, LANES), F32),
            pltpu.VMEM((2, 2, 1024, LANES), F32),
            pltpu.VMEM((4096, LANES), F32),
            pltpu.VMEM((2, 1024, LANES), F32),
            pltpu.VMEM((2, 2, 1024, LANES), F32),
            pltpu.VMEM((2, 2048, LANES), F32),
            pltpu.VMEM((REACH, SIZE), F32),
            pltpu.VMEM((2, REACH, SIZE), F32),
            pltpu.VMEM((2, 64, LANES), F32),
            pltpu.VMEM((2, 128, LANES), F32),
            pltpu.VMEM((2, 128, LANES), F32),
            pltpu.SemaphoreType.DMA((12,)),
            pltpu.SemaphoreType.DMA,
            pltpu.SemaphoreType.DMA((2,)),
            pltpu.SemaphoreType.DMA,
            pltpu.SemaphoreType.DMA((2,)),
            pltpu.SemaphoreType.DMA,
            pltpu.SemaphoreType.DMA((2,)),
            pltpu.SemaphoreType.DMA,
            pltpu.SemaphoreType.DMA,
        ],
        compiler_params=pltpu.CompilerParams(
            collective_id=0, has_side_effects=True, vmem_limit_bytes=60 << 20
        ),
        name="middle",
    )(heights, wind_cols, wind_rows, screens, strips, *of_y, *of_x)
    return pl.pallas_call(
        last_kernel,
        out_shape=(
            jax.ShapeDtypeStruct((2, REACH, SIZE), F32),
            jax.ShapeDtypeStruct((1, SPAN, SIZE), F32),
        ),
        in_specs=[smem] * 2 + [anywhere] * 4,
        out_specs=(anywhere, anywhere),
        scratch_shapes=[
            pltpu.VMEM((REACH + SPAN, SIZE), F32),
            pltpu.VMEM((1, SPAN, SIZE), F32),
            pltpu.VMEM((2, REACH, SIZE), F32),
            pltpu.SemaphoreType.DMA((4,)),
        ],
        compiler_params=pltpu.CompilerParams(vmem_limit_bytes=60 << 20),
        name="last",
    )(wind_cols, wind_rows, field, came, screens, strips)


def solution(mesh):
    placed = (P("layer", "col", None), P("layer", None, None), P(), P(), P())
    return jax.shard_map(
        on_device,
        mesh=mesh,
        in_specs=placed,
        out_specs=(P(None, ("col", "layer"), None), P("layer", "col", None)),
        check_vma=False,
    )
```

```python
import functools
import math

import jax
import jax.numpy as jnp
import numpy as np
from jax import lax
from jax.experimental import pallas as pl
from jax.experimental.pallas import tpu as pltpu
from jax.sharding import PartitionSpec as P

MESH = pl.DeviceIdType.MESH
F32 = jnp.float32
BF16 = jnp.bfloat16

SIZE = 8192
LANES = 128
SPAN = 64
REACH = 32
CHIPS = 128
DEVICES = 256
STEPS = 8
EARLY = 32
ORDER = (1, 7, 2, 6, 3, 5, 4, 0)


def cut(table):
    high = table.astype(np.float32).astype(BF16)
    low = (table - high.astype(np.float64)).astype(np.float32).astype(BF16)
    return high, low


def dft(count, sign):
    index = np.arange(count)
    return np.exp(sign * 2j * np.pi * (np.outer(index, index) % count) / count)


def left_complex(table):
    return np.block([[table.real, -table.imag], [table.imag, table.real]])


def right_complex(table):
    return np.block([[table.real, table.imag], [-table.imag, table.real]])


def left_half(table):
    high, low = cut(left_complex(table))
    return np.block([[high, high], [low, np.zeros_like(low)]])


def left_full(table):
    high, low = cut(left_complex(table))
    return np.concatenate([high, low, high], 1)


def right_full(table):
    high, low = cut(right_complex(table))
    return np.concatenate([high, low, high], 0)


def tables_y():
    twiddle = np.exp(-2j * np.pi * np.outer(np.arange(64), np.arange(128)) / SIZE)
    return [
        left_half(dft(64, -1)),
        left_half(dft(64, 1)),
        right_full(dft(128, -1)),
        right_full(dft(128, 1)),
        np.stack([twiddle.real, twiddle.imag]).astype(np.float32),
    ]


def tables_x():
    twiddle = np.exp(-2j * np.pi * np.outer(np.arange(128), np.arange(64)) / SIZE)
    twiddle = np.concatenate([twiddle, twiddle], 1)
    pair = np.eye(2)
    return [
        left_full(dft(128, -1)),
        left_full(dft(128, 1)),
        right_full(np.kron(pair, dft(64, -1))),
        right_full(np.kron(pair, dft(64, 1))),
        np.stack([twiddle.real, twiddle.imag]).astype(np.float32),
    ]


def wave(angle):
    square = angle * angle
    sine = -1.9515295891e-4 * square + 8.3321608736e-3
    sine = sine * square - 1.6666654611e-1
    sine = sine * square * angle + angle
    cosine = 2.443315711809948e-5 * square - 1.388731625493765e-3
    cosine = cosine * square + 4.166664568298827e-2
    cosine = cosine * square * square - 0.5 * square + 1.0
    return cosine, sine


def turned(cosine, sine, quarter):
    odd = (quarter & 1) == 1
    first = jnp.where(odd, sine, cosine)
    second = jnp.where(odd, cosine, sine)
    first = jnp.where(((quarter + 1) & 2) == 2, -first, first)
    second = jnp.where((quarter & 2) == 2, -second, second)
    return first, second


def cos_sin(angle):
    count = jnp.floor(angle * (2.0 / math.pi) + 0.5)
    rest = angle - count * 1.5703125
    rest = rest - count * 4.837512969970703125e-4
    rest = rest - count * 7.54978995489188216e-8
    cosine, sine = wave(rest)
    return turned(cosine, sine, count.astype(jnp.int32))


def symbol(frequency, distance, shift):
    signed = jnp.where(frequency < SIZE // 2, frequency, frequency - SIZE)
    count = (distance * signed * signed + shift * signed * SIZE) & (SIZE * SIZE - 1)
    unit = SIZE * SIZE // 4
    quarter = (count + unit // 2) // unit
    rest = (count - quarter * unit).astype(F32) * (2.0 * math.pi / (SIZE * SIZE))
    cosine, sine = wave(rest)
    cosine, sine = turned(cosine, sine, quarter)
    return cosine * (1.0 / SIZE), sine * (-1.0 / SIZE)


def split(value):
    high = value.astype(BF16)
    low = (value - high.astype(F32)).astype(BF16)
    return high, low


def dot(left, right):
    return jnp.dot(left, right, preferred_element_type=F32)


def apply_left_half(table, value):
    high, low = split(value)
    both = dot(table, jnp.concatenate([high, low], 0))
    rows = both.shape[0] // 2
    return both[:rows] + both[rows:]


def apply_left(table, value):
    high, low = split(value)
    return dot(table, jnp.concatenate([high, high, low], 0))


def apply_right(value, table):
    high, low = split(value)
    return dot(jnp.concatenate([high, high, low], 1), table)


def times(real, imag, other_real, other_imag):
    return (
        real * other_real - imag * other_imag,
        real * other_imag + imag * other_real,
    )


def symbol_y(ref, distance, shift):
    rows = lax.broadcasted_iota(jnp.int32, (64, 128), 0)
    lanes = lax.broadcasted_iota(jnp.int32, (64, 128), 1)
    ref[0], ref[1] = symbol(rows + 64 * lanes, distance, shift)


def symbol_x(ref, distance, shift):
    rows = lax.broadcasted_iota(jnp.int32, (128, 128), 0)
    lanes = lax.broadcasted_iota(jnp.int32, (128, 128), 1)
    ref[0], ref[1] = symbol(rows + 128 * (lanes % 64), distance, shift)


def along_y(src, dst, width, tables, phase):
    fwd_left, inv_left, fwd_right, inv_right, twiddle = tables
    together = 16

    def body(group, carry):
        first = group * together
        fields = []
        for i in range(together):
            rows = pl.ds(first + i, 64, stride=width)
            fields.append(jnp.concatenate([src[0, rows, :], src[1, rows, :]], 0))
        value = apply_left_half(fwd_left[...], jnp.concatenate(fields, 1))
        tw_real, tw_imag = twiddle[0], twiddle[1]
        pieces = []
        for i in range(together):
            lanes = slice(i * 128, (i + 1) * 128)
            pieces.append(
                jnp.concatenate(
                    times(value[:64, lanes], value[64:, lanes], tw_real, tw_imag), 1
                )
            )
        value = apply_right(jnp.concatenate(pieces, 0), fwd_right[...])
        ph_real, ph_imag = phase[0], phase[1]
        pieces = []
        for i in range(together):
            rows = slice(i * 64, (i + 1) * 64)
            pieces.append(
                jnp.concatenate(
                    times(value[rows, :128], value[rows, 128:], ph_real, ph_imag), 1
                )
            )
        value = apply_right(jnp.concatenate(pieces, 0), inv_right[...])
        fields = []
        for i in range(together):
            rows = slice(i * 64, (i + 1) * 64)
            fields.append(
                jnp.concatenate(
                    times(value[rows, :128], value[rows, 128:], tw_real, -tw_imag), 0
                )
            )
        value = apply_left_half(inv_left[...], jnp.concatenate(fields, 1))
        for i in range(together):
            rows = pl.ds(first + i, 64, stride=width)
            lanes = slice(i * 128, (i + 1) * 128)
            dst[0, rows, :] = value[:64, lanes]
            dst[1, rows, :] = value[64:, lanes]
        return carry

    lax.fori_loop(0, width // together, body, 0)


def along_x(fields, tables, phase):
    fwd_left, inv_left, fwd_right, inv_right, twiddle = tables
    tw_real, tw_imag = twiddle[0], twiddle[1]
    value = jnp.concatenate([jnp.concatenate(pair, 0) for pair in fields], 1)
    value = apply_left(fwd_left[...], value)
    pieces = []
    for i in range(len(fields)):
        lanes = slice(i * 128, (i + 1) * 128)
        pieces.append(
            jnp.concatenate(
                times(value[:128, lanes], value[128:, lanes], tw_real, tw_imag), 1
            )
        )
    value = apply_right(jnp.concatenate(pieces, 0), fwd_right[...])
    ph_real, ph_imag = phase[0], phase[1]
    pieces = []
    for i in range(len(fields)):
        rows = slice(i * 128, (i + 1) * 128)
        pieces.append(
            jnp.concatenate(
                times(value[rows, :128], value[rows, 128:], ph_real, ph_imag), 1
            )
        )
    value = apply_right(jnp.concatenate(pieces, 0), inv_right[...])
    pieces = []
    for i in range(len(fields)):
        rows = slice(i * 128, (i + 1) * 128)
        pieces.append(
            jnp.concatenate(
                times(value[rows, :128], value[rows, 128:], tw_real, -tw_imag), 0
            )
        )
    value = apply_left(inv_left[...], jnp.concatenate(pieces, 1))
    return [
        (value[:128, i * 128 : (i + 1) * 128], value[128:, i * 128 : (i + 1) * 128])
        for i in range(len(fields))
    ]


def every_chip(chip, visit):
    x, y, z = chip // 32, (chip // 8) % 4, chip % 8
    along_z = [(z + step) % 8 for step in ORDER]

    def plane(step, carry):
        base = ((x + step // 4) % 4) * 32 + ((y + step % 4) % 4) * 8
        for steps, place in zip(ORDER, along_z):
            visit(base + place, step == 0 if steps == 0 else None)
        return carry

    lax.fori_loop(0, 16, plane, 0)


def send_all(core, source, landing, send_sem, recv_sem):
    def remote(goal, goal_core):
        pltpu.make_async_remote_copy(
            source(goal, goal_core),
            landing,
            send_sem,
            recv_sem,
            device_id=(goal, goal_core),
            device_id_type=MESH,
        ).start()

    def visit(goal, own_chip):
        for goal_core in range(2):
            if own_chip is None:
                remote(goal, goal_core)
                continue
            own = jnp.logical_and(own_chip, core == goal_core)

            @pl.when(jnp.logical_not(own))
            def _():
                remote(goal, goal_core)

            @pl.when(own)
            def _():
                pltpu.make_async_copy(
                    source(goal, goal_core), landing, recv_sem
                ).start()

    return visit


def drain(view, sem):
    pltpu.make_async_copy(view, view, sem).wait()


def tables_in(sources, places, sems, first):
    copies = [
        pltpu.make_async_copy(source, place, sems.at[first + i])
        for i, (source, place) in enumerate(zip(sources, places))
    ]
    for copy in copies:
        copy.start()
    return copies


def middle_kernel(
    heights,
    wind_cols,
    wind_rows,
    *refs,
):
    screen_hbm, strip_hbm = refs[:2]
    tables_hbm = refs[2:12]
    out_hbm, came_hbm = refs[12:14]
    screen, strip = refs[14:16]
    tables = refs[16:26]
    (
        work,
        field_out,
        field_in,
        screen_out,
        screen_in,
        back_out,
        back_in,
        came,
        out,
        phase_y,
        phase_a,
        phase_b,
        load_sems,
        field_send,
        field_recv,
        screen_send,
        screen_recv,
        back_send,
        back_recv,
        halo_send,
        halo_recv,
    ) = refs[26:]
    chip = lax.axis_index("col")
    core = lax.axis_index("layer")
    device = chip * 2 + core
    tables_of_y, tables_of_x = tables[:5], tables[5:]

    loads = tables_in(
        (screen_hbm.at[0], strip_hbm.at[0]) + tuple(tables_hbm),
        (screen, strip) + tuple(tables),
        load_sems,
        0,
    )

    barrier = pltpu.get_barrier_semaphore()

    def greet(goal, own_chip):
        def signal(goal_core):
            pl.semaphore_signal(
                barrier, inc=1, device_id=(goal, goal_core), device_id_type=MESH
            )

        if own_chip is None:
            signal(core)
        else:
            pl.when(jnp.logical_not(own_chip))(lambda: signal(core))
        signal(1 - core)

    every_chip(chip, greet)

    least = REACH - wind_cols[core]
    row = lax.broadcasted_iota(jnp.int32, (REACH, LANES), 0)
    fresh = jnp.logical_and(chip == CHIPS - 1, row >= least)

    def unmoved(tile):
        lanes = pl.ds(pl.multiple_of(tile * LANES, LANES), LANES)
        edge = jnp.where(fresh, strip[:, lanes], screen[pl.ds(REACH, REACH), lanes])
        return jnp.concatenate([screen[pl.ds(0, REACH), lanes], edge], 0)

    for copy in loads:
        copy.wait()

    @pl.when(core == 0)
    def _():
        symbol_y(phase_y, heights[0], wind_rows[0] - wind_rows[1])

        def start(tile, carry):
            rows = pl.ds(pl.multiple_of(tile * SPAN, SPAN), SPAN)
            work[0, rows, :], work[1, rows, :] = cos_sin(unmoved(tile))
            return carry

        lax.fori_loop(0, 64, start, 0)

    @pl.when(core == 1)
    def _():
        def turn(tile, carry):
            rows = pl.ds(pl.multiple_of(tile * LANES, LANES), LANES)
            both = jnp.concatenate([unmoved(tile), unmoved(tile + 32)], 0)
            screen_out[rows, :] = both.T
            return carry

        lax.fori_loop(0, 32, turn, 0)

    pl.semaphore_wait(barrier, DEVICES - 1)

    slot = pl.ds(pl.multiple_of(chip * 8, 8), 8)

    def pass_edge(tile, carry):
        lanes = pl.ds(pl.multiple_of(tile * LANES, LANES), LANES)
        pltpu.make_async_remote_copy(
            screen.at[pl.ds(REACH, REACH), lanes],
            came.at[:, lanes],
            halo_send,
            halo_recv,
            device_id=((chip + 1) % CHIPS, core),
            device_id_type=MESH,
        ).start()
        return carry

    @pl.when(core == 0)
    def _():
        lax.fori_loop(0, EARLY, pass_edge, 0)
        along_y(work, work, SPAN, tables_of_y, phase_y)

        def turn(tile, carry):
            rows = pl.ds(pl.multiple_of(tile * LANES, LANES), LANES)
            lower = pl.ds(pl.multiple_of(tile * SPAN, SPAN), SPAN)
            upper = pl.ds(pl.multiple_of((tile + 32) * SPAN, SPAN), SPAN)
            for part in range(2):
                both = jnp.concatenate([work[part, lower, :], work[part, upper, :]], 0)
                field_out[part, rows, :] = both.T
            return carry

        lax.fori_loop(0, 32, turn, 0)

        def send(half, carry):
            def source(goal, goal_core):
                rows = pl.ds(pl.multiple_of((goal * 2 + goal_core) * 8, 8), 8)
                return field_out.reshape(2, 2, 2048, LANES).at[:, half, rows, :]

            landing = field_in.at[:, half, slot, :]
            every_chip(chip, send_all(core, source, landing, field_send, field_recv.at[half]))
            return carry

        lax.fori_loop(0, 2, send, 0)

    @pl.when(core == 1)
    def _():
        def send(half, carry):
            def source(goal, goal_core):
                rows = pl.ds(pl.multiple_of((goal * 2 + goal_core) * 8, 8), 8)
                return screen_out.reshape(2, 2048, LANES).at[half, rows, :]

            landing = screen_in.at[half, slot, :]
            every_chip(chip, send_all(core, source, landing, screen_send, screen_recv.at[half]))
            return carry

        lax.fori_loop(0, 2, send, 0)
        lax.fori_loop(0, EARLY, pass_edge, 0)

    symbol_x(phase_a, heights[0], wind_cols[0] - wind_cols[1])
    symbol_x(phase_b, heights[1], wind_cols[1])

    lane = lax.broadcasted_iota(jnp.int32, (CHIPS, LANES), 1)
    odd = (lane // 32) % 2 == 1
    own = pl.ds(pl.multiple_of(device * 8, 8), 8)

    def half_of(half, carry):
        drain(screen_in.at[half], screen_recv.at[half])
        drain(field_in.at[:, half], field_recv.at[half])

        def rows_of(step, carry):
            slabs = [pl.ds(step * 4 + i, CHIPS, stride=STEPS) for i in range(4)]
            fields = [
                (field_in[0, half, rows, :], field_in[1, half, rows, :])
                for rows in slabs
            ]
            fields = along_x(fields, tables_of_x, phase_a)
            fields = [
                times(*field, *cos_sin(screen_in[half, rows, :]))
                for field, rows in zip(fields, slabs)
            ]
            fields = along_x(fields, tables_of_x, phase_b)
            for (real, imag), rows in zip(fields, slabs):
                back_out[half, 0, rows, :] = jnp.where(odd, pltpu.roll(imag, 32, 1), real)
                back_out[half, 1, rows, :] = jnp.where(odd, imag, pltpu.roll(real, 96, 1))
            return carry

        lax.fori_loop(0, 2, rows_of, 0)

        def source(goal, goal_core):
            rows = pl.ds(pl.multiple_of(goal * 8, 8), 8)
            return back_out.at[half, goal_core, rows, :]

        landing = back_in.at[half, own, :]
        every_chip(chip, send_all(core, source, landing, back_send, back_recv.at[half]))
        return carry

    lax.fori_loop(0, 2, half_of, 0)

    lax.fori_loop(EARLY, 64, pass_edge, 0)

    symbol_y(phase_y, heights[1], wind_rows[1])

    def lanes_of(tile):
        return pl.ds(pl.multiple_of(tile * LANES, LANES), LANES)

    @pl.when(core == 0)
    def _():
        sent = field_out.reshape(2, 2, 2048, LANES).at[:, :, pl.ds(0, 2040), :]
        drain(sent, field_send)

    @pl.when(core == 1)
    def _():
        sent = screen_out.reshape(2, 2048, LANES).at[:, pl.ds(0, 2040), :]
        drain(sent, screen_send)

    for half in range(2):
        drain(back_in.at[half], back_recv.at[half])

        def turn_back(tile, carry):
            rows = pl.ds(pl.multiple_of(tile * LANES, LANES), LANES)
            tile_turned = back_in[half, rows, :].T
            for upper in range(2):
                goal = pl.multiple_of((upper * 32 + half * 16 + tile) * 32, 32)
                for part in range(2):
                    first = (upper * 2 + part) * 32
                    work[part, pl.ds(goal, 32), :] = tile_turned[first : first + 32]
            return carry

        lax.fori_loop(0, 16, turn_back, 0)
    along_y(work, work, 32, tables_of_y, phase_y)

    def finish(tile, carry):
        rows = pl.ds(pl.multiple_of(tile * 32, 32), 32)
        for part in range(2):
            out[part, :, lanes_of(tile)] = work[part, rows, :]
        return carry

    lax.fori_loop(0, 64, finish, 0)
    result = pltpu.make_async_copy(out, out_hbm, load_sems.at[1])
    result.start()

    drain(came, halo_recv)

    keep = pltpu.make_async_copy(came, came_hbm, load_sems.at[0])
    keep.start()
    drain(came, halo_send)
    drain(back_in.at[:, pl.ds(0, 2040), :], back_send)
    result.wait()
    keep.wait()


def last_kernel(wind_cols, wind_rows, *refs):
    field_hbm, came_hbm, screen_hbm, strip_hbm, out_hbm, next_hbm = refs[:6]
    extended, moved, field, sems = refs[6:]
    chip = lax.axis_index("col")
    core = lax.axis_index("layer")

    edge = extended.at[pl.ds(0, REACH)]
    screen_copy = pltpu.make_async_copy(
        screen_hbm.at[0], extended.at[pl.ds(REACH, SPAN)], sems.at[0]
    )
    screen_copy.start()

    @pl.when(chip == 0)
    def _():
        pltpu.make_async_copy(strip_hbm.at[0], edge, sems.at[1]).start()

    @pl.when(chip != 0)
    def _():
        pltpu.make_async_copy(came_hbm, edge, sems.at[1]).start()

    field_copy = pltpu.make_async_copy(field_hbm, field, sems.at[2])
    field_copy.start()
    screen_copy.wait()
    pltpu.make_async_copy(came_hbm, edge, sems.at[1]).wait()

    up = (SPAN + wind_cols[core]) % (SPAN + REACH)
    shift = wind_rows[core] & (SIZE - 1)
    tiles, within = shift // LANES, shift % LANES
    kept = lax.broadcasted_iota(jnp.int32, (SPAN, LANES), 1) >= within

    def source(tile):
        lanes = pl.ds(pl.multiple_of(((tile - tiles) & 63) * LANES, LANES), LANES)
        block = pltpu.roll(extended[:, lanes], up, 0)[:SPAN]
        return pltpu.roll(block, within, 1)

    def move(group, before):
        for i in range(8):
            tile = group * 8 + i
            here = source(tile)
            lanes = pl.ds(pl.multiple_of(tile * LANES, LANES), LANES)
            moved[0, :, lanes] = jnp.where(kept, here, before)
            before = here
        return before

    field_copy.wait()
    out_copy = pltpu.make_async_copy(field, out_hbm, sems.at[2])
    out_copy.start()
    lax.fori_loop(0, 8, move, source(-1))
    next_copy = pltpu.make_async_copy(moved, next_hbm, sems.at[3])
    next_copy.start()
    out_copy.wait()
    next_copy.wait()


def on_device(screens, strips, wind_cols, wind_rows, heights):
    of_y = [jnp.asarray(table) for table in tables_y()]
    of_x = [jnp.asarray(table) for table in tables_x()]
    smem = pl.BlockSpec(memory_space=pltpu.SMEM)
    anywhere = pl.BlockSpec(memory_space=pl.ANY)
    places_y = [pltpu.VMEM(table.shape, table.dtype) for table in of_y]
    places_x = [pltpu.VMEM(table.shape, table.dtype) for table in of_x]
    field, came = pl.pallas_call(
        middle_kernel,
        out_shape=(
            jax.ShapeDtypeStruct((2, REACH, SIZE), F32),
            jax.ShapeDtypeStruct((REACH, SIZE), F32),
        ),
        in_specs=[smem] * 3 + [anywhere] * 12,
        out_specs=(anywhere, anywhere),
        scratch_shapes=[
            pltpu.VMEM((SPAN, SIZE), F32),
            pltpu.VMEM((REACH, SIZE), F32),
        ]
        + places_y
        + places_x
        + [
            pltpu.VMEM((2, 4096, LANES), F32),
            pltpu.VMEM((2, 4096, LANES), F32),
            pltpu.VMEM((2, 2, 1024, LANES), F32),
            pltpu.VMEM((4096, LANES), F32),
            pltpu.VMEM((2, 1024, LANES), F32),
            pltpu.VMEM((2, 2, 1024, LANES), F32),
            pltpu.VMEM((2, 2048, LANES), F32),
            pltpu.VMEM((REACH, SIZE), F32),
            pltpu.VMEM((2, REACH, SIZE), F32),
            pltpu.VMEM((2, 64, LANES), F32),
            pltpu.VMEM((2, 128, LANES), F32),
            pltpu.VMEM((2, 128, LANES), F32),
            pltpu.SemaphoreType.DMA((12,)),
            pltpu.SemaphoreType.DMA,
            pltpu.SemaphoreType.DMA((2,)),
            pltpu.SemaphoreType.DMA,
            pltpu.SemaphoreType.DMA((2,)),
            pltpu.SemaphoreType.DMA,
            pltpu.SemaphoreType.DMA((2,)),
            pltpu.SemaphoreType.DMA,
            pltpu.SemaphoreType.DMA,
        ],
        compiler_params=pltpu.CompilerParams(
            collective_id=0, has_side_effects=True, vmem_limit_bytes=60 << 20
        ),
        name="middle",
    )(heights, wind_cols, wind_rows, screens, strips, *of_y, *of_x)
    return pl.pallas_call(
        last_kernel,
        out_shape=(
            jax.ShapeDtypeStruct((2, REACH, SIZE), F32),
            jax.ShapeDtypeStruct((1, SPAN, SIZE), F32),
        ),
        in_specs=[smem] * 2 + [anywhere] * 4,
        out_specs=(anywhere, anywhere),
        scratch_shapes=[
            pltpu.VMEM((REACH + SPAN, SIZE), F32),
            pltpu.VMEM((1, SPAN, SIZE), F32),
            pltpu.VMEM((2, REACH, SIZE), F32),
            pltpu.SemaphoreType.DMA((4,)),
        ],
        compiler_params=pltpu.CompilerParams(vmem_limit_bytes=60 << 20),
        name="last",
    )(wind_cols, wind_rows, field, came, screens, strips)


def solution(mesh):
    placed = (P("layer", "col", None), P("layer", None, None), P(), P(), P())
    return jax.shard_map(
        on_device,
        mesh=mesh,
        in_specs=placed,
        out_specs=(P(None, ("col", "layer"), None), P("layer", "col", None)),
        check_vma=False,
    )
```
